128 devices in a mesh: section: 4 (over x), dp: 16 (over z, y), tensor: 2 (over core).
Axes of the slice: x: 4, y: 4, z: 4, core: 2. Of those that a mesh axis runs over, the one named last changes fastest.
Arguments:
- latent_states: bfloat16 [4, 16, 512, 1, 5120], P('section', 'dp', 'tensor'), may hold values from -6 to 6
- piece_extents: int32 [4, 16, 1, 4], P('section', 'dp'), may hold values from 1 to 256, 512 in all within a row
- retained_bundles: int32 [3, 16], replicated, may hold values from -1 to 15, as said below
- mixer_scaling_factor: bfloat16 [4, 5120], P('section'), may hold values from 0.099609375 to 1.8984375
- asker_projector: bfloat16 [4, 5120, 3072], P('section', None, 'tensor')
- asker_offset_vector: bfloat16 [4, 3072], P('section', 'tensor'), may hold values from -3 to 3
- lookup_projector: bfloat16 [4, 5120, 1024], P('section', None, 'tensor'), may hold values from -0.078125 to 0.078125
- content_projector: bfloat16 [4, 5120, 1024], P('section', None, 'tensor'), may hold values from -0.078125 to 0.078125
- content_offset_vector: bfloat16 [4, 1024], P('section', 'tensor'), may hold values from -3 to 3
- mixer_output_matrix: bfloat16 [4, 3072, 5120], P('section', 'tensor'), may hold values from -0.109375 to 0.109375
- leave_rating_matrix: bfloat16 [4, 5120], P('section'), may hold values from -0.078125 to 0.078125
Outputs:
- scores: float32 [4, 16, 1, 4], P('section', 'dp')
- next_hidden: bfloat16 [4, 16, 512, 1, 5120], P('section', 'dp', 'tensor')
The draws below stay inside these ranges and needn't reach their ends.
Inputs may be any that keep to these rules, and one draw needn't show every extreme that they name: retained_bundles[s] lists in increasing order the numbers of the packs of phase s that pass its exit, then -1 entries; its k-th entry fills the pack numbered k of phase s + 1.
All inputs are finite; a program needn't handle non-finite values.
Results may differ from the reference program's by a relative error of at most 0.013.
The reference program's roundings to bfloat16 on the way (of `normed`, `query`, `keys`, `values`, `probs`, `mixed` and `phase_out`) count: a program that leaves them out, or rounds other values in their place, can miss the bound.
Values may be sent and summed in bfloat16 or wider, within the bound.
No kernel may reach another device: no remote copies, remote signals or barrier semaphores. Data moves between devices by JAX's collectives and lax.ppermute only.
A program may use at most 256 MiB of HBM per device.

```python
import math
import jax
import jax.numpy as jnp
import numpy as np
from jax import lax

D = 5120
KV = 8
QPER = 3
HD = 128
PAIR = 512
SEGS = 4
SLOTS = 1
SECTIONS = 4
GROUPS = 16
PACKS = 16
N_TENSOR = 2


def draw_retained_bundles(key, part):
    key = jax.random.fold_in(key, 11)
    passing = jax.random.randint(key, (SECTIONS - 1, PACKS), 0, 4) > 0
    numbers = jnp.arange(PACKS, dtype=jnp.int32)
    rows = jnp.arange(SECTIONS - 1, dtype=jnp.int32) % 3
    cutoff = jnp.where(rows == 0, (GROUPS - 1) * SLOTS, jnp.where(rows == 1, GROUPS // 2 * SLOTS, 0)).astype(jnp.int32)
    passing = passing & (numbers[None, :] >= cutoff[:, None])
    passing = passing | (numbers[None, :] == cutoff[:, None])
    passing = passing.at[:, PACKS - 1].set(True)
    ranking = jnp.where(passing, numbers[None, :], numbers[None, :] + PACKS)
    ordered = jnp.argsort(ranking, axis=1).astype(jnp.int32)
    counted = jnp.sum(passing.astype(jnp.int32), axis=1, keepdims=True)
    return jnp.where(numbers[None, :] < counted, ordered, -1).astype(jnp.int32)


def draw_asker_projector(key, part):
    key = jax.random.fold_in(key, 23)
    shape = (SECTIONS, D, KV * QPER * HD)
    return (jax.random.normal(key, shape, jnp.float32) * D ** (-0.5)).astype(jnp.bfloat16)


def steps_of(own_key, extent, shards, least, largest):
    factor_of = 1.0
    for position, blocks in shards:
        heights = jax.random.uniform(jax.random.fold_in(jax.random.fold_in(own_key, 6), position), (blocks,), jnp.float32, least / len(shards), largest / len(shards))
        factor_of = factor_of * jnp.repeat(jnp.exp(heights), extent[position] // blocks).reshape((-1,) + (1,) * (len(extent) - 1 - position))
    return factor_of


def split_up(number_of, total, most, slope):
    loads = [(1 << 20) // math.isqrt(rank ** slope) + 1 for rank in range(2, number_of + 1)]
    surplus, holding = total - most - (number_of - 1), [1] * (number_of - 1)
    while surplus > 0:
        movable = [i for i in range(number_of - 1) if holding[i] < most]
        mass, left = sum([loads[i] for i in movable]), surplus
        for i in movable:
            more = min(most - holding[i], max(1, left * loads[i] // mass), surplus)
            holding[i] = holding[i] + more
            surplus = surplus - more
    return np.array([most] + holding)


def uneven(stream_key, amount, total, bound, lean):
    if amount == 2:
        one = jax.random.randint(stream_key, (), max(1, total - bound), min(bound, total - 1) + 1)
        return jnp.stack([one, total - one])
    sizes = jnp.asarray(split_up(amount, total, bound, lean), jnp.int32)
    twos = (amount - 1) // 2
    giver, taker = sizes[1:1 + 2 * twos:2], sizes[2:2 + 2 * twos:2]
    slack = jnp.minimum(giver - 1, bound - taker)
    moved = jax.random.randint(jax.random.fold_in(stream_key, 1), (twos,), 0, 1 << 20) % (slack + 1)
    sizes = sizes.at[1:1 + 2 * twos:2].set(giver - moved).at[2:2 + 2 * twos:2].set(taker + moved)
    return sizes[jax.random.permutation(jax.random.fold_in(stream_key, 2), amount)]


def gaussian(key, shape, scale, bound, cuts=(), kind=jnp.bfloat16):
    result = jax.random.normal(key, shape, jnp.float32) * scale
    if len(cuts) > 0:
        result = steps_of(key, shape, cuts, -0.22, 0.18) * result
    return jnp.clip(result, min=-bound, max=bound).astype(kind)


def setup_inputs(seed: int = 0) -> dict:
    splits = jax.random.split(jax.random.key(seed), 12)
    return {
        "latent_states": gaussian(splits[0], (SECTIONS, GROUPS, PAIR, SLOTS, D), 1.0, 6.0, ((0, 4), (1, 16), (2, 2))),
        "piece_extents": jax.vmap(lambda own: uneven(own, SEGS, PAIR, PAIR // 2, 2))(jax.random.split(splits[1], SECTIONS * GROUPS * SLOTS)).reshape((SECTIONS, GROUPS, SLOTS, SEGS)).astype(jnp.int32),
        "retained_bundles": draw_retained_bundles(jax.random.fold_in(splits[11], 71), 0),
        "mixer_scaling_factor": jnp.clip(1.0 + 0.18 * jax.random.normal(splits[3], (SECTIONS, D), jnp.float32), 0.099609375, 1.8984375).astype(jnp.bfloat16),
        "asker_projector": draw_asker_projector(jax.random.fold_in(splits[11], 71), 0),
        "asker_offset_vector": gaussian(splits[5], (SECTIONS, KV * QPER * HD), 0.5, 3.0, ((0, 4), (1, 2))),
        "lookup_projector": gaussian(splits[6], (SECTIONS, D, KV * HD), D ** -0.5, 0.078125, ((0, 4), (2, 2))),
        "content_projector": gaussian(splits[7], (SECTIONS, D, KV * HD), D ** -0.5, 0.078125, ((0, 4), (2, 2))),
        "content_offset_vector": gaussian(splits[8], (SECTIONS, KV * HD), 0.5, 3.0, ((0, 4), (1, 2))),
        "mixer_output_matrix": gaussian(splits[9], (SECTIONS, KV * QPER * HD, D), (KV * QPER * HD) ** -0.5, 0.109375, ((0, 4), (1, 2))),
        "leave_rating_matrix": gaussian(splits[10], (SECTIONS, D), D ** -0.5, 0.078125, ((0, 4),)),
    }


epsilon = 1e-06
rope_base = 1000000.0

def segment_layout(lengths, length):
    ends = jnp.cumsum(lengths, axis=-1).astype(jnp.int32)
    starts = ends - lengths
    places = jnp.arange(length, dtype=jnp.int32)
    segment = lax.optimization_barrier(jnp.sum((places[:, None] >= ends[..., None, :]).astype(jnp.int32), axis=-1))
    member = (segment[..., None] == jnp.arange(lengths.shape[-1], dtype=jnp.int32)).astype(jnp.int32)
    offset = places - lax.optimization_barrier(jnp.sum(member * starts[..., None, :], axis=-1))
    return (segment, offset, ends - 1)

def rotate(vectors, angle):
    half = vectors.shape[-1] // 2
    first = vectors[..., :half]
    second = vectors[..., half:]
    cosine = jnp.cos(angle)
    sine = jnp.sin(angle)
    return jnp.concatenate([first * cosine - second * sine, second * cosine + first * sine], axis=-1)

def frequencies(width):
    return jnp.exp(-jnp.log(rope_base) * jnp.arange(0, width, 2, dtype=jnp.float32) / width)

def row_norm(vectors):
    return vectors * lax.rsqrt(lax.optimization_barrier(jnp.mean(vectors * vectors, axis=-1, keepdims=True)) + epsilon)

def phase_layer(packed, lengths, gain, w_query, q_shift, w_key, w_value, v_shift, w_out, w_score):
    hidden_f = packed.astype(jnp.float32)
    normed = (row_norm(hidden_f) * gain.astype(jnp.float32)).astype(jnp.bfloat16)
    segment, offset, last = segment_layout(lengths, PAIR)
    angle = offset.astype(jnp.float32)[:, None] * frequencies(HD)[None, :]
    query = jnp.dot(normed, w_query, preferred_element_type=jnp.float32) + q_shift.astype(jnp.float32)
    query = rotate(query.reshape(PAIR, KV, QPER, HD), angle[:, None, None, :]).astype(jnp.bfloat16)
    keys = jnp.dot(normed, w_key, preferred_element_type=jnp.float32).reshape(PAIR, KV, HD)
    keys = rotate(keys, angle[:, None, :]).astype(jnp.bfloat16)
    values = jnp.dot(normed, w_value, preferred_element_type=jnp.float32) + v_shift.astype(jnp.float32)
    values = values.astype(jnp.bfloat16).reshape(PAIR, KV, HD)
    logits = jnp.einsum('qgph,kgh->gpqk', query.astype(jnp.float32), keys.astype(jnp.float32)) * HD ** (-0.5)
    places = jnp.arange(PAIR, dtype=jnp.int32)
    allowed = (segment[:, None] == segment[None, :]) & (places[None, :] <= places[:, None])
    logits = jnp.where(allowed, logits, -1e+30)
    peak = lax.optimization_barrier(jnp.max(logits, axis=-1, keepdims=True))
    expons = jnp.exp(logits - peak)
    probs = (expons / lax.optimization_barrier(jnp.sum(expons, axis=-1, keepdims=True))).astype(jnp.bfloat16)
    mixed = jnp.einsum('gpqk,kgh->qgph', probs.astype(jnp.float32), values.astype(jnp.float32))
    mixed = mixed.astype(jnp.bfloat16).reshape(PAIR, KV * QPER * HD)
    group_width = KV * QPER * HD // N_TENSOR
    terms = jnp.einsum('ltc,tcd->tld', mixed.reshape(PAIR, N_TENSOR, group_width).astype(jnp.float32), w_out.reshape(N_TENSOR, group_width, D).astype(jnp.float32))
    terms = lax.optimization_barrier(terms.astype(jnp.bfloat16)).astype(jnp.float32)
    summed = hidden_f + lax.optimization_barrier(jnp.sum(terms, axis=0))
    row_scores = lax.optimization_barrier(jnp.sum(row_norm(summed) * w_score.astype(jnp.float32), axis=-1))
    return (summed.astype(jnp.bfloat16), jnp.take(row_scores, last, axis=0))

def reference(latent_states, piece_extents, retained_bundles, mixer_scaling_factor, asker_projector, asker_offset_vector, lookup_projector, content_projector, content_offset_vector, mixer_output_matrix, leave_rating_matrix):
    outputs = []
    exits = []
    for round_ordinal in range(SECTIONS):
        packs = jnp.transpose(latent_states[round_ordinal], (0, 2, 1, 3)).reshape(PACKS, PAIR, D)
        lengths = piece_extents[round_ordinal].reshape(PACKS, SEGS)

        def run_pack(element):
            return phase_layer(element[0], element[1], mixer_scaling_factor[round_ordinal], asker_projector[round_ordinal], asker_offset_vector[round_ordinal], lookup_projector[round_ordinal], content_projector[round_ordinal], content_offset_vector[round_ordinal], mixer_output_matrix[round_ordinal], leave_rating_matrix[round_ordinal])
        produced, graded = lax.map(run_pack, (packs, lengths))
        outputs.append(produced)
        exits.append(graded)
    phase_out = jnp.stack(outputs)
    arrived = [jnp.zeros((PACKS, PAIR, D), jnp.bfloat16)]
    for round_ordinal in range(1, SECTIONS):
        demanded_lines = retained_bundles[round_ordinal - 1]
        chosen = jnp.take(phase_out[round_ordinal - 1], jnp.maximum(demanded_lines, 0), axis=0)
        arrived.append(jnp.where((demanded_lines >= 0)[:, None, None], chosen, jnp.zeros_like(chosen)))
    next_hidden = jnp.stack(arrived).reshape(SECTIONS, GROUPS, SLOTS, PAIR, D).transpose(0, 1, 3, 2, 4)
    scores = jnp.stack(exits).reshape(SECTIONS, GROUPS, SLOTS, SEGS)
    return (scores, next_hidden)
```

```python
import jax
import jax.numpy as jnp
from jax import lax
from jax.sharding import PartitionSpec as P

HD = 128
CHUNKS = 2


epsilon = 1e-06
rope_base = 1000000.0


def segment_layout(lengths, length):
    ends = jnp.cumsum(lengths, axis=-1)
    starts = ends - lengths
    places = jnp.arange(length, dtype=jnp.int32)
    segment = jnp.sum((places[:, None] >= ends[..., None, :]).astype(jnp.int32), axis=-1)
    member = (segment[..., None] == jnp.arange(lengths.shape[-1], dtype=jnp.int32)).astype(
        jnp.int32
    )
    offset = places - jnp.sum(member * starts[..., None, :], axis=-1)
    return (segment, offset, ends - 1)


def rotate(vectors, angle):
    half = vectors.shape[-1] // 2
    first = vectors[..., :half]
    second = vectors[..., half:]
    cosine = jnp.cos(angle)
    sine = jnp.sin(angle)
    return jnp.concatenate(
        [first * cosine - second * sine, second * cosine + first * sine], axis=-1
    )


def frequencies(width):
    return jnp.exp(-jnp.log(rope_base) * jnp.arange(0, width, 2, dtype=jnp.float32) / width)


def row_norm(vectors):
    return vectors * lax.rsqrt(jnp.mean(vectors * vectors, axis=-1, keepdims=True) + epsilon)


def swap(value):
    return lax.ppermute(value, "tensor", [(0, 1), (1, 0)])


def on_device(
    latent_states,
    piece_extents,
    retained_bundles,
    mixer_scaling_factor,
    asker_projector,
    asker_offset_vector,
    lookup_projector,
    content_projector,
    content_offset_vector,
    mixer_output_matrix,
    leave_rating_matrix,
):
    local = latent_states[0, 0, :, 0]
    rows, width = local.shape
    tensor = lax.axis_index("tensor")
    section = lax.axis_index("section")
    n_dp = lax.axis_size("dp")
    pair_len = rows * 2
    hidden_f = local.astype(jnp.float32)
    normed = (row_norm(hidden_f) * mixer_scaling_factor[0].astype(jnp.float32)).astype(jnp.bfloat16)
    w_query = asker_projector[0]
    w_key = lookup_projector[0]
    w_value = content_projector[0]
    q_width = w_query.shape[1]
    k_width = w_key.shape[1]
    kv_here = k_width // HD
    q_group = q_width // k_width
    q_shift = asker_offset_vector[0].astype(jnp.float32)
    v_shift = content_offset_vector[0].astype(jnp.float32)
    other = swap(normed)
    first = jnp.where(tensor == 0, normed, other)
    second = jnp.where(tensor == 0, other, normed)
    piece = jnp.concatenate([first, second], axis=0)
    query = jnp.dot(piece, w_query, preferred_element_type=jnp.float32) + q_shift
    keys = jnp.dot(piece, w_key, preferred_element_type=jnp.float32)
    values = (jnp.dot(piece, w_value, preferred_element_type=jnp.float32) + v_shift).astype(
        jnp.bfloat16
    )
    segment, offset, last = segment_layout(piece_extents[0, 0, 0], pair_len)
    angle = offset.astype(jnp.float32)[:, None] * frequencies(HD)
    query = rotate(query.reshape(pair_len, kv_here, q_group, HD), angle[:, None, None, :])
    query = query.astype(jnp.bfloat16)
    keys = rotate(keys.reshape(pair_len, kv_here, HD), angle[:, None, :]).astype(jnp.bfloat16)
    values = values.reshape(pair_len, kv_here, HD)
    logits = jnp.einsum(
        "qgph,kgh->gpqk", query, keys, preferred_element_type=jnp.float32
    ) * HD ** (-0.5)
    places = jnp.arange(pair_len, dtype=jnp.int32)
    allowed = (segment[:, None] == segment[None, :]) & (places[None, :] <= places[:, None])
    logits = jnp.where(allowed, logits, -1e30)
    peak = jnp.max(logits, axis=-1, keepdims=True)
    expons = jnp.exp(logits - peak)
    probs = (expons / jnp.sum(expons, axis=-1, keepdims=True)).astype(jnp.bfloat16)
    mixed = jnp.einsum("gpqk,kgh->qgph", probs, values, preferred_element_type=jnp.float32)
    mixed = mixed.astype(jnp.bfloat16).reshape(pair_len, q_width)
    w_out = mixer_output_matrix[0]
    rating = leave_rating_matrix[0].astype(jnp.float32)

    wanted = lax.dynamic_index_in_dim(
        retained_bundles, jnp.minimum(section, retained_bundles.shape[0] - 1), 0, keepdims=False
    )
    forward = [(s, s + 1) for s in range(lax.axis_size("section") - 1)]
    step = width // CHUNKS
    squares = 0.0
    graded = 0.0
    arrived = []
    for c in range(CHUNKS):
        span = slice(c * step, (c + 1) * step)
        term = jnp.dot(mixed, w_out[:, span], preferred_element_type=jnp.float32).astype(
            jnp.bfloat16
        )
        mine = lax.dynamic_slice_in_dim(term, tensor * rows, rows, 0)
        theirs = lax.dynamic_slice_in_dim(term, (1 - tensor) * rows, rows, 0)
        received = swap(theirs)
        summed = hidden_f[:, span] + (mine.astype(jnp.float32) + received.astype(jnp.float32))
        squares = squares + jnp.sum(summed * summed, axis=-1)
        graded = graded + jnp.sum(summed * rating[span], axis=-1)
        out = summed.astype(jnp.bfloat16).reshape(n_dp, rows // n_dp, step)
        spread = lax.all_to_all(out, "dp", 0, 0)
        chosen = jnp.take(spread, jnp.maximum(wanted, 0), axis=0)
        chosen = jnp.where((wanted >= 0)[:, None, None], chosen, jnp.zeros_like(chosen))
        moved = lax.ppermute(chosen, "section", forward)
        arrived.append(lax.all_to_all(moved, "dp", 0, 0).reshape(rows, step))
    row_scores = graded * lax.rsqrt(squares / width + epsilon)
    global_rows = tensor * rows + jnp.arange(rows, dtype=jnp.int32)
    picked = global_rows[:, None] == last[None, :]
    partial_scores = jnp.sum(jnp.where(picked, row_scores[:, None], 0.0), axis=0)
    seg_scores = lax.psum(partial_scores, "tensor")
    arrived = jnp.concatenate(arrived, axis=1)
    return (seg_scores[None, None, None], arrived[None, None, :, None, :])


def solution(mesh):
    return jax.shard_map(
        on_device,
        mesh=mesh,
        in_specs=(
            P("section", "dp", "tensor", None, None),
            P("section", "dp", None, None),
            P(),
            P("section", None),
            P("section", None, "tensor"),
            P("section", "tensor"),
            P("section", None, "tensor"),
            P("section", None, "tensor"),
            P("section", "tensor"),
            P("section", "tensor", None),
            P("section", None),
        ),
        out_specs=(P("section", "dp", None, None), P("section", "dp", "tensor", None, None)),
        check_vma=False,
    )
```

```python
import functools
import jax
import jax.numpy as jnp
from jax import lax
from jax.experimental import pallas as pl
from jax.experimental.pallas import tpu as pltpu
from jax.sharding import PartitionSpec as P

HD = 128
TILE = 512
AHEAD = 8
CHUNKS = (3072, 2048)
VMEM = 60 * 1024 * 1024

epsilon = 1e-06
rope_base = 1000000.0


def ends_of(lengths):
    ends = []
    total = 0
    for i in range(lengths.shape[0]):
        total = total + lengths[i]
        ends.append(total)
    return ends


def starts_at(places, ends):
    start = jnp.zeros_like(places)
    for end in ends[:-1]:
        start = jnp.where(places >= end, end, start)
    return start


def swap(value):
    return lax.ppermute(value, "tensor", [(0, 1), (1, 0)])


def qkv_kernel(half, lengths, gain_ref, q_bias_ref, v_bias_ref, x, wq, wk, wv, *rest):
    out, held, normed, weights, ready, turns, x_sems, w_sems, out_sems = rest[-9:]
    rows, width = x.shape
    slots, deep = weights.shape[:2]
    tiles = []
    for source in (wq, wk, wv):
        for at in range(0, source.shape[1], TILE):
            tiles.append((source, at))
    n_query = wq.shape[1] // TILE
    n_rope = n_query + wk.shape[1] // TILE
    few = rows // 4
    parts = width // deep
    total = len(tiles) * parts

    def x_copy(r):
        here = pl.ds(r * few, few)
        return pltpu.make_async_copy(x.at[here], held.at[here], x_sems.at[r])

    def w_copy(j):
        source, at = tiles[j // parts]
        d = j % parts
        return pltpu.make_async_copy(
            source.at[d * deep : (d + 1) * deep, at : at + TILE],
            weights.at[j % slots],
            w_sems.at[j % slots],
        )

    def out_copy(t):
        return pltpu.make_async_copy(
            ready.at[:, t * TILE : (t + 1) * TILE],
            out.at[
                pl.ds(pl.multiple_of(half[0] * rows, rows), rows), t * TILE : (t + 1) * TILE
            ],
            out_sems.at[t],
        )

    for r in range(4):
        x_copy(r).start()
    for j in range(parts):
        w_copy(j).start()
    places = half[0] * rows + lax.broadcasted_iota(jnp.int32, (rows, HD), 0)
    offset = (places - starts_at(places, ends_of(lengths))).astype(jnp.float32)
    lane = lax.broadcasted_iota(jnp.int32, (1, HD), 1)
    order = (lane % (HD // 2)).astype(jnp.float32) * 2.0
    angle = offset * jnp.exp(-jnp.log(rope_base) * order / HD)
    turns[0] = jnp.cos(angle)
    turns[1] = jnp.where(lane < HD // 2, -1.0, 1.0) * jnp.sin(angle)
    for r in range(4):
        x_copy(r).wait()
        if r == 0:
            for j in range(parts, AHEAD):
                w_copy(j).start()
        for at in range(r * few, (r + 1) * few, 16):
            v = held[at : at + 16, :].astype(jnp.float32)
            factor = lax.rsqrt(jnp.mean(v * v, axis=-1, keepdims=True) + epsilon)
            normed[at : at + 16, :] = (
                v * factor * gain_ref[...].astype(jnp.float32)
            ).astype(jnp.bfloat16)

    for t in range(len(tiles)):
        for d in range(parts):
            w_copy(t * parts + d).wait()
        for j in range(t * parts + AHEAD, min((t + 1) * parts + AHEAD, total)):
            w_copy(j).start()
        part = None
        for d in range(parts):
            term = jnp.dot(
                normed[:, d * deep : (d + 1) * deep],
                weights[(t * parts + d) % slots],
                preferred_element_type=jnp.float32,
            )
            part = term if part is None else part + term
        here = slice(t * TILE, (t + 1) * TILE)
        if t < n_query:
            part = part + q_bias_ref[:, here].astype(jnp.float32)
        elif t >= n_rope:
            there = slice((t - n_rope) * TILE, (t - n_rope + 1) * TILE)
            part = part + v_bias_ref[:, there].astype(jnp.float32)
        if t < n_rope:
            for at in range(0, TILE, HD):
                u = part[:, at : at + HD]
                turned = u * turns[0] + pltpu.roll(u, HD // 2, 1) * turns[1]
                ready[:, t * TILE + at : t * TILE + at + HD] = turned.astype(jnp.bfloat16)
        else:
            ready[:, here] = part.astype(jnp.bfloat16)
        out_copy(t).start()
    for t in range(len(tiles)):
        out_copy(t).wait()


def qkv_half(half, lengths, x, gain, q_bias, v_bias, wq, wk, wv, held):
    rows, width = x.shape
    columns = wq.shape[1] + wk.shape[1] + wv.shape[1]
    n = columns // TILE
    whole = pl.BlockSpec(memory_space=pltpu.HBM)
    operands = [gain, q_bias, v_bias, x, wq, wk, wv]
    specs = [pl.BlockSpec(v.shape, lambda i, h, l: (0, 0)) for v in operands[:3]] + [whole] * 4
    aliases = {}
    if held is not None:
        operands.append(held)
        specs.append(whole)
        aliases = {len(operands) + 1: 0}
    return pl.pallas_call(
        qkv_kernel,
        grid_spec=pltpu.PrefetchScalarGridSpec(
            num_scalar_prefetch=2,
            grid=(1,),
            in_specs=specs,
            out_specs=whole,
            scratch_shapes=[
                pltpu.VMEM((rows, width), jnp.bfloat16),
                pltpu.VMEM((rows, width), jnp.bfloat16),
                pltpu.VMEM((AHEAD + 5, width // 5, TILE), jnp.bfloat16),
                pltpu.VMEM((rows, columns), jnp.bfloat16),
                pltpu.VMEM((2, rows, HD), jnp.float32),
                pltpu.SemaphoreType.DMA((4,)),
                pltpu.SemaphoreType.DMA((AHEAD + 5,)),
                pltpu.SemaphoreType.DMA((n,)),
            ],
        ),
        out_shape=jax.ShapeDtypeStruct((2 * rows, columns), jnp.bfloat16),
        input_output_aliases=aliases,
        compiler_params=pltpu.CompilerParams(vmem_limit_bytes=VMEM),
        cost_estimate=pl.CostEstimate(
            flops=2 * rows * width * columns,
            bytes_accessed=2 * width * columns,
            transcendentals=0,
        ),
        name="qkv",
    )(half, lengths, *operands)


def attention_kernel(lengths, q_ref, k_ref, v_ref, out_ref):
    ends = ends_of(lengths)
    length = k_ref.shape[0]
    groups = k_ref.shape[1] // HD
    heads = q_ref.shape[1] // HD // groups
    block = 128
    for i in range(length // block):
        lo = max(0, i - 2) * block
        hi = (i + 1) * block
        here = slice(i * block, hi)
        b = lo + lax.broadcasted_iota(jnp.int32, (hi - lo, block), 0)
        a = i * block + lax.broadcasted_iota(jnp.int32, (hi - lo, block), 1)
        start = starts_at(i * block + lax.broadcasted_iota(jnp.int32, (1, block), 1), ends)
        allowed = (b <= a) & (b >= start)
        allowed = jnp.concatenate([allowed] * heads, axis=1)
        for g in range(groups):
            at = g * HD
            q = jnp.concatenate([q_ref[here, (g * heads + h) * HD : (g * heads + h + 1) * HD] for h in range(heads)], axis=0)
            logits = lax.dot_general(
                k_ref[lo:hi, at:at+HD], q, (((1,), (1,)), ((), ())), preferred_element_type=jnp.float32
            ) * HD ** (-0.5)
            logits = jnp.where(allowed, logits, -1e30)
            expons = jnp.exp(logits - jnp.max(logits, axis=0, keepdims=True))
            probs = expons * (1.0 / jnp.sum(expons, axis=0, keepdims=True))
            mixed = lax.dot_general(
                probs.astype(jnp.bfloat16), v_ref[lo:hi, at:at+HD], (((0,), (0,)), ((), ())), preferred_element_type=jnp.float32
            ).astype(jnp.bfloat16)
            for h in range(heads):
                out_ref[here, (g * heads + h) * HD : (g * heads + h + 1) * HD] = mixed[h * block : (h + 1) * block]


def attention(lengths, qkv, q_width, k_width):
    length = qkv.shape[0]
    pace = 2
    groups = k_width // HD
    steps = groups // pace
    wide = q_width // steps
    deep = k_width // steps
    return pl.pallas_call(
        attention_kernel,
        grid_spec=pltpu.PrefetchScalarGridSpec(
            num_scalar_prefetch=1,
            grid=(steps,),
            in_specs=[
                pl.BlockSpec((length, wide), lambda g, l: (0, g)),
                pl.BlockSpec((length, deep), lambda g, l: (0, q_width // deep + g)),
                pl.BlockSpec((length, deep), lambda g, l: (0, (q_width + k_width) // deep + g)),
            ],
            out_specs=pl.BlockSpec((length, wide), lambda g, l: (0, g)),
        ),
        out_shape=jax.ShapeDtypeStruct((length, q_width), jnp.bfloat16),
        compiler_params=pltpu.CompilerParams(vmem_limit_bytes=VMEM),
        cost_estimate=pl.CostEstimate(
            flops=8 * length * length * q_width,
            bytes_accessed=8 * length * q_width,
            transcendentals=length * length,
        ),
        name="attention",
    )(lengths, qkv, qkv, qkv)


def out_kernel(at, half, mixed, w, mine, theirs, held, weights, term, m_sems, w_sems, out_sems):
    length, depth = mixed.shape
    rows, wide = mine.shape
    few, deep = length // 4, depth // 3

    def m_copy(r):
        here = slice(r * few, (r + 1) * few)
        return pltpu.make_async_copy(mixed.at[here], held.at[here], m_sems.at[r])

    def w_copies(t):
        return [
            pltpu.make_async_copy(
                w.at[d * deep : (d + 1) * deep, at + t * TILE : at + (t + 1) * TILE],
                weights.at[t, d * deep : (d + 1) * deep],
                w_sems.at[t, d],
            )
            for d in range(3)
        ]

    def out_copies(t):
        here = slice(t * TILE, (t + 1) * TILE)
        return [
            pltpu.make_async_copy(
                term.at[pl.ds(pl.multiple_of(place * rows, rows), rows), here],
                target.at[:, here],
                out_sems.at[t, i],
            )
            for i, (place, target) in enumerate(((1 - half[0], theirs), (half[0], mine)))
        ]

    n = wide // TILE
    for r in range(4):
        m_copy(r).start()
    for t in range(n):
        for copy in w_copies(t):
            copy.start()
    for r in range(4):
        m_copy(r).wait()
    for t in range(n):
        for copy in w_copies(t):
            copy.wait()
        term[:, t * TILE : (t + 1) * TILE] = jnp.dot(
            held[...], weights[t], preferred_element_type=jnp.float32
        ).astype(jnp.bfloat16)
        for copy in out_copies(t):
            copy.start()
    for t in range(n):
        for copy in out_copies(t):
            copy.wait()


def out_project(half, mixed, w_out, at, wide):
    length, depth = mixed.shape
    n = wide // TILE
    result = jax.ShapeDtypeStruct((length // 2, wide), jnp.bfloat16)
    whole = pl.BlockSpec(memory_space=pltpu.HBM)
    return pl.pallas_call(
        functools.partial(out_kernel, at),
        grid_spec=pltpu.PrefetchScalarGridSpec(
            num_scalar_prefetch=1,
            grid=(1,),
            in_specs=[whole, whole],
            out_specs=[whole, whole],
            scratch_shapes=[
                pltpu.VMEM((length, depth), jnp.bfloat16),
                pltpu.VMEM((n, depth, TILE), jnp.bfloat16),
                pltpu.VMEM((length, wide), jnp.bfloat16),
                pltpu.SemaphoreType.DMA((4,)),
                pltpu.SemaphoreType.DMA((n, 3)),
                pltpu.SemaphoreType.DMA((n, 2)),
            ],
        ),
        out_shape=[result, result],
        compiler_params=pltpu.CompilerParams(vmem_limit_bytes=VMEM),
        cost_estimate=pl.CostEstimate(
            flops=2 * length * depth * wide,
            bytes_accessed=2 * depth * wide,
            transcendentals=0,
        ),
        name="out_project",
    )(half, mixed, w_out)


def score_kernel(half, lengths, rating_ref, x, *rest):
    n = len(CHUNKS)
    mines, theirs, (out_ref, held, terms, sems) = rest[:n], rest[n : 2 * n], rest[2 * n :]
    rows, width = x.shape
    last = [end - 1 - half[0] * rows for end in ends_of(lengths)]

    def copies(i):
        row = jnp.clip(last[i], 0, rows - 1)
        here = pl.ds(pl.multiple_of(row // 16 * 16, 16), 16)
        result = [pltpu.make_async_copy(x.at[here], held.at[i], sems.at[i, 0])]
        at = 0
        for c, wide in enumerate(CHUNKS):
            for j, source in enumerate((mines[c], theirs[c])):
                result.append(
                    pltpu.make_async_copy(
                        source.at[here],
                        terms.at[j, i, :, at : at + wide],
                        sems.at[i, 1 + 2 * c + j],
                    )
                )
            at += wide
        return result

    count = held.shape[0]
    for i in range(count):
        for copy in copies(i):
            copy.start()
    out_ref[...] = jnp.zeros_like(out_ref)
    for i in range(count):
        for copy in copies(i):
            copy.wait()
        summed = held[i].astype(jnp.float32) + (
            terms[0, i].astype(jnp.float32) + terms[1, i].astype(jnp.float32)
        )
        squares = jnp.sum(summed * summed, axis=-1, keepdims=True) / width
        graded = jnp.sum(summed * rating_ref[...].astype(jnp.float32), axis=-1, keepdims=True)
        graded = graded * lax.rsqrt(squares + epsilon)
        place = lax.broadcasted_iota(jnp.int32, graded.shape, 0)
        wanted = (place == last[i] % 16) & (last[i] >= 0) & (last[i] < rows)
        graded = jnp.sum(jnp.where(wanted, graded, 0.0), axis=0, keepdims=True)
        out_ref[i : i + 1, :] = jnp.broadcast_to(graded, (1, out_ref.shape[1]))


def score(half, lengths, rating, x, mines, theirs):
    width = x.shape[1]
    count = lengths.shape[0]
    whole = pl.BlockSpec(memory_space=pltpu.HBM)
    n = 2 * len(mines)
    return pl.pallas_call(
        score_kernel,
        grid_spec=pltpu.PrefetchScalarGridSpec(
            num_scalar_prefetch=2,
            grid=(1,),
            in_specs=[pl.BlockSpec((1, width), lambda i, h, l: (0, 0)), whole] + [whole] * n,
            out_specs=pl.BlockSpec((8, 128), lambda i, h, l: (0, 0)),
            scratch_shapes=[
                pltpu.VMEM((count, 16, width), jnp.bfloat16),
                pltpu.VMEM((2, count, 16, width), jnp.bfloat16),
                pltpu.SemaphoreType.DMA((count, n + 1)),
            ],
        ),
        out_shape=jax.ShapeDtypeStruct((8, 128), jnp.float32),
        compiler_params=pltpu.CompilerParams(vmem_limit_bytes=VMEM),
        cost_estimate=pl.CostEstimate(
            flops=8 * 64 * width, bytes_accessed=6 * 64 * width, transcendentals=0
        ),
        name="score",
    )(half, lengths, rating, x, *mines, *theirs)


def choose_kernel(phase, retained, spread, chosen, held, in_sems, out_sems):
    packs = chosen.shape[0]
    wanted = [retained[jnp.minimum(phase[0], retained.shape[0] - 1), k] for k in range(packs)]

    def fetch(k):
        source = spread.at[jnp.clip(wanted[k], 0, packs - 1)]
        return pltpu.make_async_copy(source, held.at[k], in_sems.at[k])

    def store(k):
        return pltpu.make_async_copy(held.at[k], chosen.at[k], out_sems.at[k])

    for k in range(packs):
        fetch(k).start()
    for k in range(packs):
        fetch(k).wait()

        @pl.when(wanted[k] < 0)
        def _():
            held[k] = jnp.zeros(held.shape[1:], held.dtype)

        store(k).start()
    for k in range(packs):
        store(k).wait()


def choose(phase, retained, spread):
    packs, rows, wide = spread.shape
    return pl.pallas_call(
        choose_kernel,
        grid_spec=pltpu.PrefetchScalarGridSpec(
            num_scalar_prefetch=2,
            grid=(1,),
            in_specs=[pl.BlockSpec(memory_space=pltpu.HBM)],
            out_specs=pl.BlockSpec(memory_space=pltpu.HBM),
            scratch_shapes=[
                pltpu.VMEM((packs, rows, wide), jnp.bfloat16),
                pltpu.SemaphoreType.DMA((packs,)),
                pltpu.SemaphoreType.DMA((packs,)),
            ],
        ),
        out_shape=jax.ShapeDtypeStruct(spread.shape, spread.dtype),
        compiler_params=pltpu.CompilerParams(vmem_limit_bytes=VMEM),
        cost_estimate=pl.CostEstimate(
            flops=0, bytes_accessed=4 * packs * rows * wide, transcendentals=0
        ),
        name="choose",
    )(phase, retained, spread)


def on_device(
    latent_states,
    piece_extents,
    retained_bundles,
    mixer_scaling_factor,
    asker_projector,
    asker_offset_vector,
    lookup_projector,
    content_projector,
    content_offset_vector,
    mixer_output_matrix,
    leave_rating_matrix,
):
    local = latent_states[0, 0, :, 0]
    rows, width = local.shape
    n_dp = lax.axis_size("dp")
    half = lax.axis_index("tensor").astype(jnp.int32).reshape(1)
    phase = lax.axis_index("section").astype(jnp.int32).reshape(1)
    lengths = piece_extents.reshape(piece_extents.shape[-1])
    w_query = asker_projector[0]
    w_key = lookup_projector[0]
    w_value = content_projector[0]
    w_out = mixer_output_matrix[0]
    operands = (
        mixer_scaling_factor,
        asker_offset_vector,
        content_offset_vector,
        w_query,
        w_key,
        w_value,
    )
    other = swap(local)
    qkv = qkv_half(half, lengths, local, *operands, None)
    qkv = qkv_half(1 - half, lengths, other, *operands, qkv)
    mixed = attention(lengths, qkv, w_query.shape[1], w_key.shape[1])

    forward = [(s, s + 1) for s in range(lax.axis_size("section") - 1)]

    def exchange(value):
        return lax.all_to_all(value, "dp", 0, 0)

    def onward(value):
        return lax.ppermute(value, "section", forward)

    mines = []
    theirs = []
    outs = []
    at = 0
    for wide in CHUNKS:
        mine, sent = out_project(half, mixed, w_out, at, wide)
        received = swap(sent)
        mines.append(mine)
        theirs.append(received)
        out = local[:, at : at + wide].astype(jnp.float32) + (
            mine.astype(jnp.float32) + received.astype(jnp.float32)
        )
        outs.append(out.astype(jnp.bfloat16).reshape(n_dp, rows // n_dp, wide))
        at += wide
    first = choose(phase, retained_bundles, exchange(outs[0]))
    moved = onward(first)
    first, second = lax.optimization_barrier((first, outs[1]))
    second = exchange(choose(phase, retained_bundles, exchange(second)))
    second, moved = lax.optimization_barrier((second, moved))
    second = onward(second)
    first = exchange(moved)
    arrived = [v.reshape(rows, v.shape[2]) for v in (first, second)]
    scores = score(half, lengths, leave_rating_matrix, local, mines, theirs)
    scores = scores[: lengths.shape[0], 0]
    seg_scores = lax.psum(scores, "tensor")
    arrived = jnp.concatenate(arrived, axis=1)
    return (seg_scores[None, None, None], arrived[None, None, :, None, :])


def solution(mesh):
    return jax.shard_map(
        on_device,
        mesh=mesh,
        in_specs=(
            P("section", "dp", "tensor", None, None),
            P("section", "dp", None, None),
            P(),
            P("section", None),
            P("section", None, "tensor"),
            P("section", "tensor"),
            P("section", None, "tensor"),
            P("section", None, "tensor"),
            P("section", "tensor"),
            P("section", "tensor", None),
            P("section", None),
        ),
        out_specs=(P("section", "dp", None, None), P("section", "dp", "tensor", None, None)),
        check_vma=False,
    )
```

```python
import functools
import jax
import jax.numpy as jnp
from jax import lax
from jax.experimental import pallas as pl
from jax.experimental.pallas import tpu as pltpu
from jax.sharding import PartitionSpec as P

HD = 128
TILE = 512
AHEAD = 8
CHUNKS = (2560, 2560)
VMEM = 60 * 1024 * 1024
COST = pl.CostEstimate(flops=1, bytes_accessed=1, transcendentals=0)

epsilon = 1e-06
rope_base = 1000000.0


def ends_of(lengths):
    ends = []
    total = 0
    for i in range(lengths.shape[0]):
        total = total + lengths[i]
        ends.append(total)
    return ends


def starts_at(places, ends):
    start = jnp.zeros_like(places)
    for end in ends[:-1]:
        start = jnp.where(places >= end, end, start)
    return start


def swap(value):
    return lax.ppermute(value, "tensor", [(0, 1), (1, 0)])


def qkv_kernel(half, lengths, gain_ref, q_bias_ref, v_bias_ref, x, other, wq, wk, wv, *rest):
    out, held, normed, weights, ready, turns, x_sems, w_sems, out_sems = rest
    rows, width = normed.shape
    few = rows // 8
    slots, deep = weights.shape[:2]
    tiles = []
    for source in (wq, wk, wv):
        for at in range(0, source.shape[1], TILE):
            tiles.append((source, at))
    n_query = wq.shape[1] // TILE
    n_rope = n_query + wk.shape[1] // TILE
    parts = width // deep
    total = len(tiles) * parts

    def x_copy(r):
        source = (x, other)[r // 4]
        here = source.at[r % 4 * few : (r % 4 + 1) * few]
        return pltpu.make_async_copy(here, held.at[r * few : (r + 1) * few], x_sems.at[r])

    def w_copy(j):
        source, at = tiles[j // parts]
        d = j % parts
        return pltpu.make_async_copy(
            source.at[d * deep : (d + 1) * deep, at : at + TILE],
            weights.at[j % slots],
            w_sems.at[j % slots],
        )

    def out_copy(t):
        return pltpu.make_async_copy(
            ready.at[:, t * TILE : (t + 1) * TILE],
            out.at[:, t * TILE : (t + 1) * TILE],
            out_sems.at[t],
        )

    for r in range(8):
        x_copy(r).start()
    for j in range(parts):
        w_copy(j).start()
    places = lax.broadcasted_iota(jnp.int32, (rows, HD), 0)
    offset = (places - starts_at(places, ends_of(lengths))).astype(jnp.float32)
    lane = lax.broadcasted_iota(jnp.int32, (1, HD), 1)
    order = (lane % (HD // 2)).astype(jnp.float32) * 2.0
    angle = offset * jnp.exp(-jnp.log(rope_base) * order / HD)
    turns[0] = jnp.cos(angle)
    turns[1] = jnp.where(lane < HD // 2, -1.0, 1.0) * jnp.sin(angle)
    for r in range(8):
        x_copy(r).wait()
        if r == 4:
            for j in range(parts, AHEAD):
                w_copy(j).start()
        shift = (r // 4 + half[0]) % 2 * (rows // 2) + r % 4 * few
        for at in range(0, few, 16):
            v = held[r * few + at : r * few + at + 16, :].astype(jnp.float32)
            factor = lax.rsqrt(jnp.mean(v * v, axis=-1, keepdims=True) + epsilon)
            normed[pl.ds(pl.multiple_of(shift + at, 16), 16), :] = (
                v * factor * gain_ref[...].astype(jnp.float32)
            ).astype(jnp.bfloat16)

    for t in range(len(tiles)):
        for d in range(parts):
            w_copy(t * parts + d).wait()
        for j in range(t * parts + AHEAD, min((t + 1) * parts + AHEAD, total)):
            w_copy(j).start()
        part = None
        for d in range(parts):
            term = jnp.dot(
                normed[:, d * deep : (d + 1) * deep],
                weights[(t * parts + d) % slots],
                preferred_element_type=jnp.float32,
            )
            part = term if part is None else part + term
        here = slice(t * TILE, (t + 1) * TILE)
        if t < n_query:
            part = part + q_bias_ref[:, here].astype(jnp.float32)
        elif t >= n_rope:
            there = slice((t - n_rope) * TILE, (t - n_rope + 1) * TILE)
            part = part + v_bias_ref[:, there].astype(jnp.float32)
        if t < n_rope:
            for at in range(0, TILE, HD):
                u = part[:, at : at + HD]
                turned = u * turns[0] + pltpu.roll(u, HD // 2, 1) * turns[1]
                ready[:, t * TILE + at : t * TILE + at + HD] = turned.astype(jnp.bfloat16)
        else:
            ready[:, here] = part.astype(jnp.bfloat16)
        out_copy(t).start()
    for t in range(len(tiles)):
        out_copy(t).wait()


def project_in(half, lengths, x, other, gain, q_bias, v_bias, wq, wk, wv):
    rows, width = 2 * x.shape[0], x.shape[1]
    columns = wq.shape[1] + wk.shape[1] + wv.shape[1]
    n = columns // TILE
    whole = pl.BlockSpec(memory_space=pltpu.HBM)
    operands = [gain, q_bias, v_bias, x, other, wq, wk, wv]
    specs = [pl.BlockSpec(v.shape, lambda i, h, l: (0, 0)) for v in operands[:3]] + [whole] * 5
    return pl.pallas_call(
        qkv_kernel,
        grid_spec=pltpu.PrefetchScalarGridSpec(
            num_scalar_prefetch=2,
            grid=(1,),
            in_specs=specs,
            out_specs=whole,
            scratch_shapes=[
                pltpu.VMEM((rows, width), jnp.bfloat16),
                pltpu.VMEM((rows, width), jnp.bfloat16),
                pltpu.VMEM((AHEAD + 5, width // 5, TILE), jnp.bfloat16),
                pltpu.VMEM((rows, columns), jnp.bfloat16),
                pltpu.VMEM((2, rows, HD), jnp.float32),
                pltpu.SemaphoreType.DMA((8,)),
                pltpu.SemaphoreType.DMA((AHEAD + 5,)),
                pltpu.SemaphoreType.DMA((n,)),
            ],
        ),
        out_shape=jax.ShapeDtypeStruct((rows, columns), jnp.bfloat16),
        compiler_params=pltpu.CompilerParams(vmem_limit_bytes=VMEM),
        cost_estimate=COST,
        name="qkv",
    )(half, lengths, *operands)


def attention_kernel(half, lengths, q_ref, k_ref, v_ref, out_ref):
    ends = ends_of(lengths)
    rows = q_ref.shape[0]
    groups = k_ref.shape[1] // HD
    heads = q_ref.shape[1] // HD // groups
    block = 128

    def rows_of(first):
        for i in range(0, rows, block):
            hi = first + i + block
            lo = max(0, hi - 3 * block)
            here = slice(i, i + block)
            b = lo + lax.broadcasted_iota(jnp.int32, (hi - lo, block), 0)
            a = hi - block + lax.broadcasted_iota(jnp.int32, (hi - lo, block), 1)
            start = starts_at(hi - block + lax.broadcasted_iota(jnp.int32, (1, block), 1), ends)
            allowed = (b <= a) & (b >= start)
            allowed = jnp.concatenate([allowed] * heads, axis=1)
            for g in range(groups):
                at = slice(g * HD, (g + 1) * HD)
                places = [slice(h * HD, (h + 1) * HD) for h in range(g * heads, (g + 1) * heads)]
                q = jnp.concatenate([q_ref[here, place] for place in places], axis=0)
                logits = lax.dot_general(
                    k_ref[lo:hi, at],
                    q,
                    (((1,), (1,)), ((), ())),
                    preferred_element_type=jnp.float32,
                ) * HD ** (-0.5)
                logits = jnp.where(allowed, logits, -1e30)
                expons = jnp.exp(logits - jnp.max(logits, axis=0, keepdims=True))
                probs = expons * (1.0 / jnp.sum(expons, axis=0, keepdims=True))
                mixed = lax.dot_general(
                    probs.astype(jnp.bfloat16),
                    v_ref[lo:hi, at],
                    (((0,), (0,)), ((), ())),
                    preferred_element_type=jnp.float32,
                ).astype(jnp.bfloat16)
                for h, place in enumerate(places):
                    out_ref[here, place] = mixed[h * block : (h + 1) * block]

    @pl.when(half[0] == 0)
    def _():
        rows_of(0)

    @pl.when(half[0] != 0)
    def _():
        rows_of(rows)


def attention(half, lengths, qkv, q_width, k_width):
    length = qkv.shape[0]
    rows = length // 2
    pace = 2
    steps = k_width // HD // pace
    wide = q_width // steps
    deep = k_width // steps
    return pl.pallas_call(
        attention_kernel,
        grid_spec=pltpu.PrefetchScalarGridSpec(
            num_scalar_prefetch=2,
            grid=(steps,),
            in_specs=[
                pl.BlockSpec((rows, wide), lambda g, h, l: (h[0], g)),
                pl.BlockSpec((length, deep), lambda g, h, l: (0, q_width // deep + g)),
                pl.BlockSpec((length, deep), lambda g, h, l: (0, (q_width + k_width) // deep + g)),
            ],
            out_specs=pl.BlockSpec((rows, wide), lambda g, h, l: (0, g)),
        ),
        out_shape=jax.ShapeDtypeStruct((rows, q_width), jnp.bfloat16),
        compiler_params=pltpu.CompilerParams(vmem_limit_bytes=VMEM),
        cost_estimate=COST,
        name="attention",
    )(half, lengths, qkv, qkv, qkv)


def choose_kernel(phase, retained, spread, chosen, held, in_sems, out_sems):
    packs, few, _ = spread.shape
    wanted = [retained[jnp.minimum(phase[0], retained.shape[0] - 1), k] for k in range(packs)]

    def fetch(k):
        source = spread.at[jnp.clip(wanted[k], 0, packs - 1)]
        return pltpu.make_async_copy(source, held.at[k * few : (k + 1) * few], in_sems.at[k])

    def store(k):
        here = slice(k * few, (k + 1) * few)
        return pltpu.make_async_copy(held.at[here], chosen.at[here], out_sems.at[k])

    for k in range(packs):
        fetch(k).start()
    for k in range(packs):
        fetch(k).wait()

        @pl.when(wanted[k] < 0)
        def _():
            held[k * few : (k + 1) * few, :] = jnp.zeros((few, held.shape[1]), held.dtype)

        store(k).start()
    for k in range(packs):
        store(k).wait()


def choose(phase, retained, spread):
    packs, few, wide = spread.shape
    whole = pl.BlockSpec(memory_space=pltpu.HBM)
    return pl.pallas_call(
        choose_kernel,
        grid_spec=pltpu.PrefetchScalarGridSpec(
            num_scalar_prefetch=2,
            grid=(1,),
            in_specs=[whole],
            out_specs=whole,
            scratch_shapes=[
                pltpu.VMEM((packs * few, wide), jnp.bfloat16),
                pltpu.SemaphoreType.DMA((packs,)),
                pltpu.SemaphoreType.DMA((packs,)),
            ],
        ),
        out_shape=jax.ShapeDtypeStruct((packs * few, wide), spread.dtype),
        compiler_params=pltpu.CompilerParams(vmem_limit_bytes=VMEM),
        cost_estimate=COST,
        name="choose",
    )(phase, retained, spread)


def out_kernel(at, phase, retained, mixed, latent, w_mine, w_theirs, out, *rest):
    held, latents, weights, ready, m_sems, l_sem, w_sems, out_sems = rest[-8:]
    rows, wide = out.shape
    width = held.shape[1]
    depth = width // 2
    n = wide // TILE

    def w_copies(t):
        here = slice(at + t * TILE, at + (t + 1) * TILE)
        return [
            pltpu.make_async_copy(source.at[:, here], weights.at[t, i], w_sems.at[t, i])
            for i, source in enumerate((w_mine, w_theirs))
        ]

    def out_copy(t):
        here = slice(t * TILE, (t + 1) * TILE)
        return pltpu.make_async_copy(ready.at[:, here], out.at[:, here], out_sems.at[t])

    l_copy = pltpu.make_async_copy(latent.at[:, at : at + wide], latents, l_sem.at[0])
    if at == 0:
        packs, few, _ = mixed.shape
        wanted = [retained[jnp.minimum(phase[0], retained.shape[0] - 1), k] for k in range(packs)]

        def m_copy(k):
            source = mixed.at[jnp.clip(wanted[k], 0, packs - 1)]
            return pltpu.make_async_copy(source, held.at[k * few : (k + 1) * few], m_sems.at[k])

        for copy in w_copies(0):
            copy.start()
        for k in range(packs):
            m_copy(k).start()
        l_copy.start()
        for k in range(packs):
            m_copy(k).wait()

            @pl.when(wanted[k] < 0)
            def _():
                held[k * few : (k + 1) * few, :] = jnp.zeros((few, width), held.dtype)

        keep = pltpu.make_async_copy(held, rest[0], m_sems.at[0])
        keep.start()
    else:
        m_copy = pltpu.make_async_copy(mixed, held, m_sems.at[0])
        m_copy.start()
        for copy in w_copies(0):
            copy.start()
        l_copy.start()
        m_copy.wait()
    for copy in w_copies(1):
        copy.start()
    for t in range(n):
        for copy in w_copies(t):
            copy.wait()
        if t + 2 < n:
            for copy in w_copies(t + 2):
                copy.start()
        here = slice(t * TILE, (t + 1) * TILE)
        branch = 0.0
        for i in range(2):
            term = jnp.dot(
                held[:, i * depth : (i + 1) * depth],
                weights[t, i],
                preferred_element_type=jnp.float32,
            )
            branch = branch + term.astype(jnp.bfloat16).astype(jnp.float32)
        if t == 0:
            l_copy.wait()
        ready[:, here] = (latents[:, here].astype(jnp.float32) + branch).astype(jnp.bfloat16)
        out_copy(t).start()
    for t in range(n):
        out_copy(t).wait()
    if at == 0:
        keep.wait()


def out_project(phase, retained, mixed, latent, w_mine, w_theirs, at, wide):
    rows = latent.shape[0]
    width = mixed.shape[-1]
    n = wide // TILE
    whole = pl.BlockSpec(memory_space=pltpu.HBM)
    result = [jax.ShapeDtypeStruct((rows, wide), jnp.bfloat16)]
    if at == 0:
        result.append(jax.ShapeDtypeStruct((rows, width), jnp.bfloat16))
    return pl.pallas_call(
        functools.partial(out_kernel, at),
        grid_spec=pltpu.PrefetchScalarGridSpec(
            num_scalar_prefetch=2,
            grid=(1,),
            in_specs=[whole] * 4,
            out_specs=[whole] * len(result),
            scratch_shapes=[
                pltpu.VMEM((rows, width), jnp.bfloat16),
                pltpu.VMEM((rows, wide), jnp.bfloat16),
                pltpu.VMEM((n, 2, width // 2, TILE), jnp.bfloat16),
                pltpu.VMEM((rows, wide), jnp.bfloat16),
                pltpu.SemaphoreType.DMA((16,)),
                pltpu.SemaphoreType.DMA((1,)),
                pltpu.SemaphoreType.DMA((n, 2)),
                pltpu.SemaphoreType.DMA((n,)),
            ],
        ),
        out_shape=result,
        compiler_params=pltpu.CompilerParams(vmem_limit_bytes=VMEM),
        cost_estimate=COST,
        name="out_project",
    )(phase, retained, mixed, latent, w_mine, w_theirs)


def terms_kernel(half, lengths, mine, theirs, w, out, held, weights, ready, m_sems, w_sems, out_sem):
    rows, depth = mine.shape
    count = lengths.shape[0]
    ends = ends_of(lengths)
    n = weights.shape[0]
    tile = weights.shape[2]

    def m_copy(i, source):
        last = jnp.clip(ends[i] - 1, 0, 2 * rows - 1)
        here = pl.ds(pl.multiple_of(last % rows // 16 * 16, 16), 16)
        return pltpu.make_async_copy(
            source.at[here], held.at[i * 16 : (i + 1) * 16], m_sems.at[i]
        )

    def w_copy(t):
        return pltpu.make_async_copy(
            w.at[:, t * tile : (t + 1) * tile], weights.at[t], w_sems.at[t]
        )

    for i in range(count):
        last = jnp.clip(ends[i] - 1, 0, 2 * rows - 1)

        @pl.when(last // rows == half[0])
        def _():
            m_copy(i, mine).start()

        @pl.when(last // rows != half[0])
        def _():
            m_copy(i, theirs).start()

    for t in range(n):
        w_copy(t).start()
    for i in range(count):
        m_copy(i, mine).wait()
    for t in range(n):
        w_copy(t).wait()
        ready[:, t * tile : (t + 1) * tile] = jnp.dot(
            held[...], weights[t], preferred_element_type=jnp.float32
        ).astype(jnp.bfloat16)
    copy = pltpu.make_async_copy(ready, out, out_sem.at[0])
    copy.start()
    copy.wait()


def score_terms(half, lengths, mine, theirs, w_out):
    depth, width = w_out.shape
    count = lengths.shape[0]
    whole = pl.BlockSpec(memory_space=pltpu.HBM)
    n = 5
    return pl.pallas_call(
        terms_kernel,
        grid_spec=pltpu.PrefetchScalarGridSpec(
            num_scalar_prefetch=2,
            grid=(1,),
            in_specs=[whole] * 3,
            out_specs=whole,
            scratch_shapes=[
                pltpu.VMEM((count * 16, depth), jnp.bfloat16),
                pltpu.VMEM((n, depth, width // n), jnp.bfloat16),
                pltpu.VMEM((count * 16, width), jnp.bfloat16),
                pltpu.SemaphoreType.DMA((count,)),
                pltpu.SemaphoreType.DMA((n,)),
                pltpu.SemaphoreType.DMA((1,)),
            ],
        ),
        out_shape=jax.ShapeDtypeStruct((count * 16, width), jnp.bfloat16),
        compiler_params=pltpu.CompilerParams(vmem_limit_bytes=VMEM),
        cost_estimate=COST,
        name="score_terms",
    )(half, lengths, mine, theirs, w_out)


def score_kernel(half, lengths, rating_ref, mine_ref, theirs_ref, x, out_ref, held, sems):
    rows, width = x.shape
    last = [end - 1 - half[0] * rows for end in ends_of(lengths)]

    def copy(i):
        row = jnp.clip(last[i], 0, rows - 1)
        here = pl.ds(pl.multiple_of(row // 16 * 16, 16), 16)
        return pltpu.make_async_copy(x.at[here], held.at[i], sems.at[i])

    count = held.shape[0]
    for i in range(count):
        copy(i).start()
    out_ref[...] = jnp.zeros_like(out_ref)
    for i in range(count):
        copy(i).wait()
        here = slice(i * 16, (i + 1) * 16)
        summed = held[i].astype(jnp.float32) + (
            mine_ref[here, :].astype(jnp.float32) + theirs_ref[here, :].astype(jnp.float32)
        )
        squares = jnp.sum(summed * summed, axis=-1, keepdims=True) / width
        graded = jnp.sum(summed * rating_ref[...].astype(jnp.float32), axis=-1, keepdims=True)
        graded = graded * lax.rsqrt(squares + epsilon)
        place = lax.broadcasted_iota(jnp.int32, graded.shape, 0)
        wanted = (place == last[i] % 16) & (last[i] >= 0) & (last[i] < rows)
        graded = jnp.sum(jnp.where(wanted, graded, 0.0), axis=0, keepdims=True)
        out_ref[i : i + 1, :] = jnp.broadcast_to(graded, (1, out_ref.shape[1]))


def score(half, lengths, rating, x, mine, theirs):
    width = x.shape[1]
    count = lengths.shape[0]
    spec = pl.BlockSpec(mine.shape, lambda i, h, l: (0, 0))
    return pl.pallas_call(
        score_kernel,
        grid_spec=pltpu.PrefetchScalarGridSpec(
            num_scalar_prefetch=2,
            grid=(1,),
            in_specs=[
                pl.BlockSpec((1, width), lambda i, h, l: (0, 0)),
                spec,
                spec,
                pl.BlockSpec(memory_space=pltpu.HBM),
            ],
            out_specs=pl.BlockSpec((8, 128), lambda i, h, l: (0, 0)),
            scratch_shapes=[
                pltpu.VMEM((count, 16, width), jnp.bfloat16),
                pltpu.SemaphoreType.DMA((count,)),
            ],
        ),
        out_shape=jax.ShapeDtypeStruct((8, 128), jnp.float32),
        compiler_params=pltpu.CompilerParams(vmem_limit_bytes=VMEM),
        cost_estimate=COST,
        name="score",
    )(half, lengths, rating, mine, theirs, x)


def on_device(
    latent_states,
    piece_extents,
    retained_bundles,
    mixer_scaling_factor,
    asker_projector,
    asker_offset_vector,
    lookup_projector,
    content_projector,
    content_offset_vector,
    mixer_output_matrix,
    leave_rating_matrix,
):
    local = latent_states[0, 0, :, 0]
    rows, width = local.shape
    n_dp = lax.axis_size("dp")
    half = lax.axis_index("tensor").astype(jnp.int32).reshape(1)
    phase = lax.axis_index("section").astype(jnp.int32).reshape(1)
    lengths = piece_extents.reshape(piece_extents.shape[-1])
    w_query = asker_projector[0]
    w_key = lookup_projector[0]
    w_value = content_projector[0]
    w_out = mixer_output_matrix[0]
    operands = (
        mixer_scaling_factor,
        asker_offset_vector,
        content_offset_vector,
        w_query,
        w_key,
        w_value,
    )
    q_width = w_query.shape[1]
    k_width = w_key.shape[1]
    forward = [(s, s + 1) for s in range(lax.axis_size("section") - 1)]

    def exchange(value):
        return lax.all_to_all(
            value.reshape(n_dp, rows // n_dp, value.shape[-1]), "dp", 0, 0
        )

    def onward(value):
        return lax.ppermute(value, "section", forward)

    q_width = w_query.shape[1]
    k_width = w_key.shape[1]
    forward = [(s, s + 1) for s in range(lax.axis_size("section") - 1)]

    def exchange(value):
        return lax.all_to_all(
            value.reshape(n_dp, rows // n_dp, value.shape[-1]), "dp", 0, 0
        )

    def onward(value):
        return lax.ppermute(value, "section", forward)

    def after(value, earlier):
        return lax.optimization_barrier((value, earlier))[0]

    other = swap(local)
    latent = exchange(local)
    w_other = swap(after(w_out, other))
    qkv = project_in(half, lengths, local, other, *operands)
    sent = attention(1 - half, lengths, qkv, q_width, k_width)
    received = swap(sent)
    mine = attention(half, lengths, qkv, q_width, k_width)
    mixed = exchange(after(jnp.concatenate([mine, received], axis=1), latent))
    latent = choose(phase, retained_bundles, latent)
    terms = score_terms(half, lengths, mine, sent, w_out)
    mixed = after(mixed, (terms, latent))

    operands = (latent, w_out, w_other)
    first, mixed = out_project(phase, retained_bundles, mixed, *operands, 0, CHUNKS[0])
    (second,) = out_project(phase, retained_bundles, mixed, *operands, *CHUNKS)
    first = onward(first)
    second = exchange(second)
    second, first = lax.optimization_barrier((second, first))
    second = onward(second)
    first = exchange(first)
    arrived = jnp.concatenate([v.reshape(rows, v.shape[-1]) for v in (first, second)], axis=1)

    received = swap(terms)
    scores = score(half, lengths, leave_rating_matrix, local, terms, received)
    seg_scores = lax.psum(scores[: lengths.shape[0], 0], "tensor")
    return (seg_scores[None, None, None], arrived[None, None, :, None, :])


def solution(mesh):
    return jax.shard_map(
        on_device,
        mesh=mesh,
        in_specs=(
            P("section", "dp", "tensor", None, None),
            P("section", "dp", None, None),
            P(),
            P("section", None),
            P("section", None, "tensor"),
            P("section", "tensor"),
            P("section", None, "tensor"),
            P("section", None, "tensor"),
            P("section", "tensor"),
            P("section", "tensor", None),
            P("section", None),
        ),
        out_specs=(P("section", "dp", None, None), P("section", "dp", "tensor", None, None)),
        check_vma=False,
    )
```

```python
import functools
import jax
import jax.numpy as jnp
from jax import lax
from jax.experimental import pallas as pl
from jax.experimental.pallas import tpu as pltpu
from jax.sharding import PartitionSpec as P

HD = 128
TILE = 512
AHEAD = 8
CHUNKS = (2560, 2560)
VMEM = 60 * 1024 * 1024
COST = pl.CostEstimate(flops=1, bytes_accessed=1, transcendentals=0)

epsilon = 1e-06
rope_base = 1000000.0


def ends_of(lengths):
    ends = []
    total = 0
    for i in range(lengths.shape[0]):
        total = total + lengths[i]
        ends.append(total)
    return ends


def starts_at(places, ends):
    start = jnp.zeros_like(places)
    for end in ends[:-1]:
        start = jnp.where(places >= end, end, start)
    return start


def swap(value):
    return lax.ppermute(value, "tensor", [(0, 1), (1, 0)])


def qkv_kernel(half, lengths, gain_ref, q_bias_ref, v_bias_ref, x, other, wq, wk, wv, *rest):
    mine, sent, held, normed, weights, ready, turns, passed, x_sems, w_sems, out_sems = rest
    rows, width = normed.shape
    few = rows // 8
    slots, deep = weights.shape[:2]
    tiles = []
    for source in (wq, wk, wv):
        for at in range(0, source.shape[1], TILE):
            tiles.append((source, at))
    n_query = wq.shape[1] // TILE
    n_rope = n_query + wk.shape[1] // TILE
    parts = width // deep
    total = len(tiles) * parts

    def x_copy(r):
        source = (x, other)[r // 4]
        here = source.at[r % 4 * few : (r % 4 + 1) * few]
        return pltpu.make_async_copy(here, held.at[r * few : (r + 1) * few], x_sems.at[r])

    def w_copy(j):
        source, at = tiles[j // parts]
        d = j % parts
        return pltpu.make_async_copy(
            source.at[d * deep : (d + 1) * deep, at : at + TILE],
            weights.at[j % slots],
            w_sems.at[j % slots],
        )

    for r in range(8):
        x_copy(r).start()
    for j in range(parts):
        w_copy(j).start()
    places = lax.broadcasted_iota(jnp.int32, (rows, HD), 0)
    offset = (places - starts_at(places, ends_of(lengths))).astype(jnp.float32)
    lane = lax.broadcasted_iota(jnp.int32, (1, HD), 1)
    order = (lane % (HD // 2)).astype(jnp.float32) * 2.0
    angle = offset * jnp.exp(-jnp.log(rope_base) * order / HD)
    turns[0] = jnp.cos(angle)
    turns[1] = jnp.where(lane < HD // 2, -1.0, 1.0) * jnp.sin(angle)
    for r in range(8):
        x_copy(r).wait()
        if r == 4:
            for j in range(parts, AHEAD):
                w_copy(j).start()
        shift = (r // 4 + half[0]) % 2 * (rows // 2) + r % 4 * few
        for at in range(0, few, 16):
            v = held[r * few + at : r * few + at + 16, :].astype(jnp.float32)
            factor = lax.rsqrt(jnp.mean(v * v, axis=-1, keepdims=True) + epsilon)
            normed[pl.ds(pl.multiple_of(shift + at, 16), 16), :] = (
                v * factor * gain_ref[...].astype(jnp.float32)
            ).astype(jnp.bfloat16)

    for t in range(len(tiles)):
        for d in range(parts):
            w_copy(t * parts + d).wait()
        for j in range(t * parts + AHEAD, min((t + 1) * parts + AHEAD, total)):
            w_copy(j).start()
        part = None
        for d in range(parts):
            term = jnp.dot(
                normed[:, d * deep : (d + 1) * deep],
                weights[(t * parts + d) % slots],
                preferred_element_type=jnp.float32,
            )
            part = term if part is None else part + term
        here = slice(t * TILE, (t + 1) * TILE)
        if t < n_query:
            part = part + q_bias_ref[:, here].astype(jnp.float32)
        elif t >= n_rope:
            there = slice((t - n_rope) * TILE, (t - n_rope + 1) * TILE)
            part = part + v_bias_ref[:, there].astype(jnp.float32)
        if t < n_rope:
            for at in range(0, TILE, HD):
                u = part[:, at : at + HD]
                turned = u * turns[0] + pltpu.roll(u, HD // 2, 1) * turns[1]
                ready[:, t * TILE + at : t * TILE + at + HD] = turned.astype(jnp.bfloat16)
        else:
            ready[:, here] = part.astype(jnp.bfloat16)

    q_width, k_width = wq.shape[1], wk.shape[1]
    ends = ends_of(lengths)
    q_ref = ready.at[:, :q_width]
    k_ref = ready.at[:, q_width : q_width + k_width]
    v_ref = ready.at[:, q_width + k_width :]

    def attend_both(sent_first, mine_first):
        for i, first in enumerate((sent_first, mine_first)):
            attend(rows // 2, first, ends, q_ref, k_ref, v_ref, passed.at[i], q_width)
            out_copy(i).start()

    def out_copy(i):
        target = (sent, mine.at[:, :q_width])[i]
        return pltpu.make_async_copy(passed.at[i], target, out_sems.at[i])

    @pl.when(half[0] == 0)
    def _():
        attend_both(rows // 2, 0)

    @pl.when(half[0] != 0)
    def _():
        attend_both(0, rows // 2)

    for i in range(2):
        out_copy(i).wait()


def project_in(half, lengths, x, other, gain, q_bias, v_bias, wq, wk, wv):
    rows, width = 2 * x.shape[0], x.shape[1]
    columns = wq.shape[1] + wk.shape[1] + wv.shape[1]
    n = columns // TILE
    whole = pl.BlockSpec(memory_space=pltpu.HBM)
    operands = [gain, q_bias, v_bias, x, other, wq, wk, wv]
    specs = [pl.BlockSpec(v.shape, lambda i, h, l: (0, 0)) for v in operands[:3]] + [whole] * 5
    return pl.pallas_call(
        qkv_kernel,
        grid_spec=pltpu.PrefetchScalarGridSpec(
            num_scalar_prefetch=2,
            grid=(1,),
            in_specs=specs,
            out_specs=[whole, whole],
            scratch_shapes=[
                pltpu.VMEM((rows, width), jnp.bfloat16),
                pltpu.VMEM((rows, width), jnp.bfloat16),
                pltpu.VMEM((AHEAD + 5, width // 5, TILE), jnp.bfloat16),
                pltpu.VMEM((rows, columns), jnp.bfloat16),
                pltpu.VMEM((2, rows, HD), jnp.float32),
                pltpu.VMEM((2, rows // 2, wq.shape[1]), jnp.bfloat16),
                pltpu.SemaphoreType.DMA((8,)),
                pltpu.SemaphoreType.DMA((AHEAD + 5,)),
                pltpu.SemaphoreType.DMA((2,)),
            ],
        ),
        out_shape=[
            jax.ShapeDtypeStruct((rows // 2, 2 * wq.shape[1]), jnp.bfloat16),
            jax.ShapeDtypeStruct((rows // 2, wq.shape[1]), jnp.bfloat16),
        ],
        compiler_params=pltpu.CompilerParams(vmem_limit_bytes=VMEM),
        cost_estimate=COST,
        name="qkv",
    )(half, lengths, *operands)


def attend(rows, first, ends, q_ref, k_ref, v_ref, out_ref, wide):
    groups = k_ref.shape[1] // HD
    heads = wide // HD // groups
    block = 128
    for i in range(0, rows, block):
        hi = first + i + block
        lo = max(0, hi - 3 * block)
        here = slice(i, i + block)
        there = slice(hi - block, hi)
        b = lo + lax.broadcasted_iota(jnp.int32, (hi - lo, block), 0)
        a = hi - block + lax.broadcasted_iota(jnp.int32, (hi - lo, block), 1)
        start = starts_at(hi - block + lax.broadcasted_iota(jnp.int32, (1, block), 1), ends)
        allowed = (b <= a) & (b >= start)
        allowed = jnp.concatenate([allowed] * heads, axis=1)
        for g in range(groups):
            at = slice(g * HD, (g + 1) * HD)
            places = [slice(h * HD, (h + 1) * HD) for h in range(g * heads, (g + 1) * heads)]
            q = jnp.concatenate([q_ref[there, place] for place in places], axis=0)
            logits = lax.dot_general(
                k_ref[lo:hi, at],
                q,
                (((1,), (1,)), ((), ())),
                preferred_element_type=jnp.float32,
            ) * HD ** (-0.5)
            logits = jnp.where(allowed, logits, -1e30)
            expons = jnp.exp(logits - jnp.max(logits, axis=0, keepdims=True))
            probs = expons * (1.0 / jnp.sum(expons, axis=0, keepdims=True))
            mixed = lax.dot_general(
                probs.astype(jnp.bfloat16),
                v_ref[lo:hi, at],
                (((0,), (0,)), ((), ())),
                preferred_element_type=jnp.float32,
            ).astype(jnp.bfloat16)
            for h, place in enumerate(places):
                out_ref[here, place] = mixed[h * block : (h + 1) * block]


def choose_kernel(phase, retained, spread, chosen, held, in_sems, out_sems):
    packs, few, _ = spread.shape
    wanted = [retained[jnp.minimum(phase[0], retained.shape[0] - 1), k] for k in range(packs)]

    def fetch(k):
        source = spread.at[jnp.clip(wanted[k], 0, packs - 1)]
        return pltpu.make_async_copy(source, held.at[k * few : (k + 1) * few], in_sems.at[k])

    def store(k):
        here = slice(k * few, (k + 1) * few)
        return pltpu.make_async_copy(held.at[here], chosen.at[here], out_sems.at[k])

    for k in range(packs):
        fetch(k).start()
    for k in range(packs):
        fetch(k).wait()

        @pl.when(wanted[k] < 0)
        def _():
            held[k * few : (k + 1) * few, :] = jnp.zeros((few, held.shape[1]), held.dtype)

        store(k).start()
    for k in range(packs):
        store(k).wait()


def choose(phase, retained, spread):
    packs, few, wide = spread.shape
    whole = pl.BlockSpec(memory_space=pltpu.HBM)
    return pl.pallas_call(
        choose_kernel,
        grid_spec=pltpu.PrefetchScalarGridSpec(
            num_scalar_prefetch=2,
            grid=(1,),
            in_specs=[whole],
            out_specs=whole,
            scratch_shapes=[
                pltpu.VMEM((packs * few, wide), jnp.bfloat16),
                pltpu.SemaphoreType.DMA((packs,)),
                pltpu.SemaphoreType.DMA((packs,)),
            ],
        ),
        out_shape=jax.ShapeDtypeStruct((packs * few, wide), spread.dtype),
        compiler_params=pltpu.CompilerParams(vmem_limit_bytes=VMEM),
        cost_estimate=COST,
        name="choose",
    )(phase, retained, spread)


def out_kernel(at, phase, retained, mixed, latent, w_mine, w_theirs, out, *rest):
    held, latents, weights, ready, m_sems, l_sem, w_sems, out_sems = rest[-8:]
    rows, wide = out.shape
    width = held.shape[1]
    depth = width // 2
    n = wide // TILE

    def w_copies(t):
        here = slice(at + t * TILE, at + (t + 1) * TILE)
        return [
            pltpu.make_async_copy(source.at[:, here], weights.at[t, i], w_sems.at[t, i])
            for i, source in enumerate((w_mine, w_theirs))
        ]

    def out_copy(t):
        here = slice(t * TILE, (t + 1) * TILE)
        return pltpu.make_async_copy(ready.at[:, here], out.at[:, here], out_sems.at[t])

    l_copy = pltpu.make_async_copy(latent.at[:, at : at + wide], latents, l_sem.at[0])
    if at == 0:
        packs, few, _ = mixed.shape
        wanted = [retained[jnp.minimum(phase[0], retained.shape[0] - 1), k] for k in range(packs)]

        def m_copy(k):
            source = mixed.at[jnp.clip(wanted[k], 0, packs - 1)]
            return pltpu.make_async_copy(source, held.at[k * few : (k + 1) * few], m_sems.at[k])

        for k in range(packs):
            m_copy(k).start()
        for copy in w_copies(0):
            copy.start()
        l_copy.start()
        for k in range(packs):
            m_copy(k).wait()

            @pl.when(wanted[k] < 0)
            def _():
                held[k * few : (k + 1) * few, :] = jnp.zeros((few, width), held.dtype)

        keep = pltpu.make_async_copy(held, rest[0], m_sems.at[0])
        keep.start()
    else:
        m_copy = pltpu.make_async_copy(mixed, held, m_sems.at[0])
        m_copy.start()
        for copy in w_copies(0):
            copy.start()
        l_copy.start()
        m_copy.wait()
    for copy in w_copies(1):
        copy.start()
    for t in range(n):
        if t + 2 < n:
            for copy in w_copies(t + 2):
                copy.start()
        here = slice(t * TILE, (t + 1) * TILE)
        branch = 0.0
        for i in range(2):
            w_copies(t)[i].wait()
            term = jnp.dot(
                held[:, i * depth : (i + 1) * depth],
                weights[t, i],
                preferred_element_type=jnp.float32,
            )
            branch = branch + term.astype(jnp.bfloat16).astype(jnp.float32)
        if t == 0:
            l_copy.wait()
        ready[:, here] = (latents[:, here].astype(jnp.float32) + branch).astype(jnp.bfloat16)
        out_copy(t).start()
    for t in range(n):
        out_copy(t).wait()
    if at == 0:
        keep.wait()


def out_project(phase, retained, mixed, latent, w_mine, w_theirs, at, wide):
    rows = latent.shape[0]
    width = mixed.shape[-1]
    n = wide // TILE
    whole = pl.BlockSpec(memory_space=pltpu.HBM)
    result = [jax.ShapeDtypeStruct((rows, wide), jnp.bfloat16)]
    if at == 0:
        result.append(jax.ShapeDtypeStruct((rows, width), jnp.bfloat16))
    return pl.pallas_call(
        functools.partial(out_kernel, at),
        grid_spec=pltpu.PrefetchScalarGridSpec(
            num_scalar_prefetch=2,
            grid=(1,),
            in_specs=[whole] * 4,
            out_specs=[whole] * len(result),
            scratch_shapes=[
                pltpu.VMEM((rows, width), jnp.bfloat16),
                pltpu.VMEM((rows, wide), jnp.bfloat16),
                pltpu.VMEM((n, 2, width // 2, TILE), jnp.bfloat16),
                pltpu.VMEM((rows, wide), jnp.bfloat16),
                pltpu.SemaphoreType.DMA((16,)),
                pltpu.SemaphoreType.DMA((1,)),
                pltpu.SemaphoreType.DMA((n, 2)),
                pltpu.SemaphoreType.DMA((n,)),
            ],
        ),
        out_shape=result,
        compiler_params=pltpu.CompilerParams(vmem_limit_bytes=VMEM),
        cost_estimate=COST,
        name="out_project",
    )(phase, retained, mixed, latent, w_mine, w_theirs)


def terms_kernel(half, lengths, mine, theirs, w, out, held, weights, ready, m_sems, w_sems, out_sem):
    rows, depth = theirs.shape
    count = lengths.shape[0]
    ends = ends_of(lengths)
    n = weights.shape[0]
    tile = weights.shape[2]

    def m_copy(i, source):
        last = jnp.clip(ends[i] - 1, 0, 2 * rows - 1)
        here = pl.ds(pl.multiple_of(last % rows // 16 * 16, 16), 16)
        return pltpu.make_async_copy(
            source.at[here, :depth], held.at[i * 16 : (i + 1) * 16], m_sems.at[i]
        )

    def w_copy(t):
        return pltpu.make_async_copy(
            w.at[:, t * tile : (t + 1) * tile], weights.at[t], w_sems.at[t]
        )

    for i in range(count):
        last = jnp.clip(ends[i] - 1, 0, 2 * rows - 1)

        @pl.when(last // rows == half[0])
        def _():
            m_copy(i, mine).start()

        @pl.when(last // rows != half[0])
        def _():
            m_copy(i, theirs).start()

    for t in range(n):
        w_copy(t).start()
    for i in range(count):
        m_copy(i, mine).wait()
    for t in range(n):
        w_copy(t).wait()
        ready[:, t * tile : (t + 1) * tile] = jnp.dot(
            held[...], weights[t], preferred_element_type=jnp.float32
        ).astype(jnp.bfloat16)
    copy = pltpu.make_async_copy(ready, out, out_sem.at[0])
    copy.start()
    copy.wait()


def score_terms(half, lengths, mine, theirs, w_out):
    depth, width = w_out.shape
    count = lengths.shape[0]
    whole = pl.BlockSpec(memory_space=pltpu.HBM)
    n = 5
    return pl.pallas_call(
        terms_kernel,
        grid_spec=pltpu.PrefetchScalarGridSpec(
            num_scalar_prefetch=2,
            grid=(1,),
            in_specs=[whole] * 3,
            out_specs=whole,
            scratch_shapes=[
                pltpu.VMEM((count * 16, depth), jnp.bfloat16),
                pltpu.VMEM((n, depth, width // n), jnp.bfloat16),
                pltpu.VMEM((count * 16, width), jnp.bfloat16),
                pltpu.SemaphoreType.DMA((count,)),
                pltpu.SemaphoreType.DMA((n,)),
                pltpu.SemaphoreType.DMA((1,)),
            ],
        ),
        out_shape=jax.ShapeDtypeStruct((count * 16, width), jnp.bfloat16),
        compiler_params=pltpu.CompilerParams(vmem_limit_bytes=VMEM),
        cost_estimate=COST,
        name="score_terms",
    )(half, lengths, mine, theirs, w_out)


def score_kernel(half, lengths, rating_ref, mine_ref, theirs_ref, x, out_ref, held, sems):
    rows, width = x.shape
    last = [end - 1 - half[0] * rows for end in ends_of(lengths)]

    def copy(i):
        row = jnp.clip(last[i], 0, rows - 1)
        here = pl.ds(pl.multiple_of(row // 16 * 16, 16), 16)
        return pltpu.make_async_copy(x.at[here], held.at[i], sems.at[i])

    count = held.shape[0]
    for i in range(count):
        copy(i).start()
    out_ref[...] = jnp.zeros_like(out_ref)
    for i in range(count):
        copy(i).wait()
        here = slice(i * 16, (i + 1) * 16)
        summed = held[i].astype(jnp.float32) + (
            mine_ref[here, :].astype(jnp.float32) + theirs_ref[here, :].astype(jnp.float32)
        )
        squares = jnp.sum(summed * summed, axis=-1, keepdims=True) / width
        graded = jnp.sum(summed * rating_ref[...].astype(jnp.float32), axis=-1, keepdims=True)
        graded = graded * lax.rsqrt(squares + epsilon)
        place = lax.broadcasted_iota(jnp.int32, graded.shape, 0)
        wanted = (place == last[i] % 16) & (last[i] >= 0) & (last[i] < rows)
        graded = jnp.sum(jnp.where(wanted, graded, 0.0), axis=0, keepdims=True)
        out_ref[i : i + 1, :] = jnp.broadcast_to(graded, (1, out_ref.shape[1]))


def score(half, lengths, rating, x, mine, theirs):
    width = x.shape[1]
    count = lengths.shape[0]
    spec = pl.BlockSpec(mine.shape, lambda i, h, l: (0, 0))
    return pl.pallas_call(
        score_kernel,
        grid_spec=pltpu.PrefetchScalarGridSpec(
            num_scalar_prefetch=2,
            grid=(1,),
            in_specs=[
                pl.BlockSpec((1, width), lambda i, h, l: (0, 0)),
                spec,
                spec,
                pl.BlockSpec(memory_space=pltpu.HBM),
            ],
            out_specs=pl.BlockSpec((8, 128), lambda i, h, l: (0, 0)),
            scratch_shapes=[
                pltpu.VMEM((count, 16, width), jnp.bfloat16),
                pltpu.SemaphoreType.DMA((count,)),
            ],
        ),
        out_shape=jax.ShapeDtypeStruct((8, 128), jnp.float32),
        compiler_params=pltpu.CompilerParams(vmem_limit_bytes=VMEM),
        cost_estimate=COST,
        name="score",
    )(half, lengths, rating, mine, theirs, x)


def on_device(
    latent_states,
    piece_extents,
    retained_bundles,
    mixer_scaling_factor,
    asker_projector,
    asker_offset_vector,
    lookup_projector,
    content_projector,
    content_offset_vector,
    mixer_output_matrix,
    leave_rating_matrix,
):
    local = latent_states[0, 0, :, 0]
    rows, width = local.shape
    n_dp = lax.axis_size("dp")
    half = lax.axis_index("tensor").astype(jnp.int32).reshape(1)
    phase = lax.axis_index("section").astype(jnp.int32).reshape(1)
    lengths = piece_extents.reshape(piece_extents.shape[-1])
    w_query = asker_projector[0]
    w_key = lookup_projector[0]
    w_value = content_projector[0]
    w_out = mixer_output_matrix[0]
    operands = (
        mixer_scaling_factor,
        asker_offset_vector,
        content_offset_vector,
        w_query,
        w_key,
        w_value,
    )
    forward = [(s, s + 1) for s in range(lax.axis_size("section") - 1)]

    def exchange(value):
        return lax.all_to_all(
            value.reshape(n_dp, rows // n_dp, value.shape[-1]), "dp", 0, 0
        )

    def onward(value):
        return lax.ppermute(value, "section", forward)

    forward = [(s, s + 1) for s in range(lax.axis_size("section") - 1)]

    def exchange(value):
        return lax.all_to_all(
            value.reshape(n_dp, rows // n_dp, value.shape[-1]), "dp", 0, 0
        )

    def onward(value):
        return lax.ppermute(value, "section", forward)

    def after(value, earlier):
        return lax.optimization_barrier((value, earlier))[0]

    other = swap(local)
    latent = exchange(local)
    mine, sent = project_in(half, lengths, local, other, *operands)
    received = swap(sent)
    mine = lax.dynamic_update_slice(mine, after(received, latent), (0, received.shape[1]))
    w_other = swap(after(w_out, mine))
    mixed = exchange(mine)
    latent = choose(phase, retained_bundles, latent)
    terms = score_terms(half, lengths, mine, sent, w_out)
    mixed = after(mixed, (terms, latent))

    operands = (latent, w_out, w_other)
    first, mixed = out_project(phase, retained_bundles, mixed, *operands, 0, CHUNKS[0])
    (second,) = out_project(phase, retained_bundles, mixed, *operands, *CHUNKS)
    first = onward(first)
    second = exchange(second)
    theirs = swap(terms)
    scores = score(half, lengths, leave_rating_matrix, local, terms, theirs)
    seg_scores = lax.psum(scores[: lengths.shape[0], 0], "tensor")
    second, first, seg_scores = lax.optimization_barrier((second, first, seg_scores))
    first = exchange(first)
    second = onward(second)
    first = lax.pad(first.reshape(rows, CHUNKS[0]), jnp.bfloat16(0), ((0, 0, 0), (0, CHUNKS[1], 0)))
    arrived = lax.dynamic_update_slice(first, second.reshape(rows, CHUNKS[1]), (0, CHUNKS[0]))

    return (seg_scores[None, None, None], arrived[None, None, :, None, :])


def solution(mesh):
    return jax.shard_map(
        on_device,
        mesh=mesh,
        in_specs=(
            P("section", "dp", "tensor", None, None),
            P("section", "dp", None, None),
            P(),
            P("section", None),
            P("section", None, "tensor"),
            P("section", "tensor"),
            P("section", None, "tensor"),
            P("section", None, "tensor"),
            P("section", "tensor"),
            P("section", "tensor", None),
            P("section", None),
        ),
        out_specs=(P("section", "dp", None, None), P("section", "dp", "tensor", None, None)),
        check_vma=False,
    )
```
